512 devices in a mesh: fsdp: 32 (over z_hi, y, core), rep: 16 (over z_lo, x).
Axes of the slice: x: 4, y: 8, z: 8 (z_hi: 2, z_lo: 4; z = z_hi * 4 + z_lo), core: 2. Of those that a mesh axis runs over, the one named last changes fastest.
Arguments:
- student_global: bfloat16 [512, 257, 768], P(('fsdp', 'rep')), may hold values from -24 to 24
- student_local: bfloat16 [1024, 37, 768], P(('fsdp', 'rep')), may hold values from -6 to 6
- teacher_global: bfloat16 [512, 257, 768], P(('fsdp', 'rep')), may hold values from -6 to 6
- grad_global: bfloat16 [512, 257, 768], P(('fsdp', 'rep')), may hold values from -6 to 6
- grad_local: bfloat16 [1024, 37, 768], P(('fsdp', 'rep')), may hold values from -6 to 6
- student_qkv: float32 [768, 2304], P('fsdp'), may hold values from -0.21875 to 0.21875
- teacher_qkv: float32 [768, 2304], P('fsdp'), may hold values from -0.21875 to 0.21875
- first_moment: float32 [768, 2304], P('fsdp'), may hold values from -1 to 1
- second_moment: float32 [768, 2304], P('fsdp'), may hold values from 1e-05 to 0.002
Outputs:
- student_out_global: bfloat16 [512, 257, 768], P(('fsdp', 'rep'))
- student_out_local: bfloat16 [1024, 37, 768], P(('fsdp', 'rep'))
- teacher_out: bfloat16 [512, 257, 768], P(('fsdp', 'rep'))
- back_global: bfloat16 [512, 257, 768], P(('fsdp', 'rep'))
- back_local: bfloat16 [1024, 37, 768], P(('fsdp', 'rep'))
- new_student: float32 [768, 2304], P('fsdp')
- new_teacher: float32 [768, 2304], P('fsdp')
- new_first: float32 [768, 2304], P('fsdp')
- new_second: float32 [768, 2304], P('fsdp')
The draws below stay inside these ranges and needn't reach their ends.
All inputs are finite; a program needn't handle non-finite values.
Results may differ from the reference program's by a relative error of at most 0.017.
Values may be sent and summed in bfloat16 or wider, within the bound.
No kernel may reach another device: no remote copies, remote signals or barrier semaphores. Data moves between devices by JAX's collectives and lax.ppermute only.
A program may use at most 64 MiB of HBM per device.

```python
import math
import jax
import jax.numpy as jnp
from jax import lax

HEADS = 12
HEAD_DIM = 64
D = 768
G_TOK = 257
L_TOK = 37
G_DEV = 1
L_DEV = 2
GLOBALS = 512
LOCALS = 1024
NTOK = 169472
N_FSDP = 32
N_REP = 16


def gradient_level():
    return math.sqrt(2.7 * (G_DEV + L_DEV) / (G_DEV * G_TOK + L_DEV * L_TOK))


def draw_first_moment(key, part):
    key = jax.random.fold_in(key, 11)
    level = 0.65 * gradient_level()
    values = jnp.clip(jax.random.normal(key, (D, 3 * D), jnp.float32), -6.0, 6.0)
    return level * values


def draw_second_moment(key, part):
    key = jax.random.fold_in(key, 23)
    level = gradient_level() ** 2
    exponent = jax.random.uniform(key, (D, 3 * D), jnp.float32, -3.0, -1.5)
    return level * jnp.exp(exponent * math.log(10.0))


def raised(array, own_key, source, target, parts, factor):
    owner, partner = [(jnp.arange(array.shape[position]) // (array.shape[position] // parts)).reshape([-1 if axis == position else 1 for axis in range(array.ndim)]) for position in (source, target)]
    chosen = jax.random.permutation(own_key, parts)[partner]
    strong = (owner == chosen) | (owner == (partner + parts // 2) % parts)
    return jnp.where(strong, factor * array, array)


def levels(key, extent, pieces, low, top_value):
    factor_of = 1.0
    for position, shards_of in pieces:
        steps = jax.random.uniform(jax.random.fold_in(jax.random.fold_in(key, 6), position), (shards_of,), jnp.float32, low / len(pieces), top_value / len(pieces))
        factor_of = factor_of * jnp.repeat(jnp.exp(steps), extent[position] // shards_of).reshape((-1,) + (1,) * (len(extent) - 1 - position))
    return factor_of


def noise(stream_key, shape, deviation, most, cuts=(), dtype=jnp.bfloat16):
    gain = levels(stream_key, shape, cuts, -0.22, 0.18) if cuts else 1.0
    array = jax.random.normal(stream_key, shape, jnp.float32) * deviation * gain
    return jnp.minimum(jnp.maximum(array, -most), most).astype(dtype)


def heavy_noise(key, extent, width, limit, split, heavy, held_as=jnp.bfloat16):
    drawn = width * jax.random.normal(key, extent, jnp.float32)
    if split:
        drawn = drawn * levels(key, extent, split, -0.22, 0.18)
    return jnp.clip(raised(drawn, jax.random.fold_in(key, 3), *heavy), -limit, limit).astype(held_as)


def setup_inputs(seed: int = 0) -> dict:
    streams_of = jax.random.split(jax.random.key(seed), 10)
    return {
        "student_global": heavy_noise(streams_of[0], (GLOBALS, G_TOK, D), 1.0, 24.0, ((0, 512),), (0, 2, 256, 6.0)),
        "student_local": noise(streams_of[1], (LOCALS, L_TOK, D), 1.0, 6.0, ((0, 512),)),
        "teacher_global": noise(streams_of[2], (GLOBALS, G_TOK, D), 1.0, 6.0, ((0, 512),)),
        "grad_global": noise(streams_of[3], (GLOBALS, G_TOK, D), 1.0, 6.0, ((0, 512),)),
        "grad_local": noise(streams_of[4], (LOCALS, L_TOK, D), 1.0, 6.0, ((0, 512),)),
        "student_qkv": noise(streams_of[5], (D, 3 * D), D ** -0.5, 0.21875, ((0, 32),), jnp.float32),
        "teacher_qkv": noise(streams_of[6], (D, 3 * D), D ** -0.5, 0.21875, ((0, 32),), jnp.float32),
        "first_moment": draw_first_moment(jax.random.fold_in(streams_of[9], 71), 0),
        "second_moment": draw_second_moment(jax.random.fold_in(streams_of[9], 71), 0),
    }


norm_eps = 1e-06
beta_one = 0.9
beta_two = 0.999
corr_one = 1.0 - 0.9 ** 10
corr_two = 1.0 - 0.999 ** 10
learn_rate = 0.002
decay_rate = 0.04
momentum = 0.994
adam_eps = 1e-08

def attend(crops, weight):
    crop_count, length, feature = crops.shape
    inputs = crops.astype(jnp.float32)
    average = lax.optimization_barrier(jnp.mean(inputs, axis=-1, keepdims=True))
    centred = inputs - average
    variance = lax.optimization_barrier(jnp.mean(centred * centred, axis=-1, keepdims=True))
    normed = (centred * lax.rsqrt(variance + norm_eps)).astype(jnp.bfloat16)
    projected = jnp.dot(normed.reshape(crop_count * length, feature), weight, preferred_element_type=jnp.float32)
    projected = projected.astype(jnp.bfloat16).reshape(crop_count, length, 3, HEADS, HEAD_DIM)
    queries = projected[:, :, 0].astype(jnp.float32)
    key_rows = projected[:, :, 1].astype(jnp.float32)
    value_rows = projected[:, :, 2].astype(jnp.float32)
    scores = jnp.einsum('nqhe,nkhe->nhqk', queries, key_rows) * HEAD_DIM ** (-0.5)
    exponent = jnp.exp(scores)
    probability = (exponent / lax.optimization_barrier(jnp.sum(exponent, axis=-1, keepdims=True))).astype(jnp.bfloat16)
    heads_out = jnp.einsum('nhqk,nkhe->nqhe', probability.astype(jnp.float32), value_rows)
    return heads_out.reshape(crop_count, length, HEADS * HEAD_DIM)

def student_pass(global_crops, local_crops, weight, cot_global, cot_local):

    def forward(global_in, local_in, weight_in):
        return (attend(global_in, weight_in), attend(local_in, weight_in))
    results, pullback = jax.vjp(forward, global_crops, local_crops, weight)
    back_g, back_l, weight_term = pullback((cot_global.astype(jnp.float32), cot_local.astype(jnp.float32)))
    return (results, back_g, back_l, weight_term)

def adam_update(weight, teacher, first, second, gradient):
    first = beta_one * first + (1.0 - beta_one) * gradient
    second = beta_two * second + (1.0 - beta_two) * gradient * gradient
    update = first / corr_one / (jnp.sqrt(second / corr_two) + adam_eps)
    weight_new = weight - learn_rate * (update + decay_rate * weight)
    teacher_new = momentum * teacher + (1.0 - momentum) * weight_new
    return (weight_new, teacher_new, first, second)

def reference(student_global, student_local, teacher_global, grad_global, grad_local, student_qkv, teacher_qkv, first_moment, second_moment):
    device_total = N_FSDP * N_REP
    student_half = student_qkv.astype(jnp.bfloat16)
    teacher_half = teacher_qkv.astype(jnp.bfloat16)
    stacked = (student_global.reshape(device_total, G_DEV, G_TOK, D), student_local.reshape(device_total, L_DEV, L_TOK, D), teacher_global.reshape(device_total, G_DEV, G_TOK, D), grad_global.reshape(device_total, G_DEV, G_TOK, D), grad_local.reshape(device_total, L_DEV, L_TOK, D))

    def per_device(carry, inputs):
        s_global, s_local, t_global, c_global, c_local = inputs
        results, back_g, back_l, weight_term = student_pass(s_global, s_local, student_half, c_global, c_local)
        teacher_rows = attend(t_global, teacher_half).astype(jnp.bfloat16)
        carry = carry + weight_term.astype(jnp.float32)
        return (carry, (results[0].astype(jnp.bfloat16), results[1].astype(jnp.bfloat16), teacher_rows, back_g, back_l))
    summed, outputs = lax.scan(per_device, jnp.zeros((D, 3 * D), jnp.float32), stacked)
    gradient = summed * (1.0 / jnp.sqrt(jnp.float32(NTOK)))
    new_student, new_teacher, new_first, new_second = adam_update(student_qkv, teacher_qkv, first_moment, second_moment, gradient)
    out_global, out_local, teacher_out, back_global, back_local = outputs
    return (out_global.reshape(GLOBALS, G_TOK, D), out_local.reshape(LOCALS, L_TOK, D), teacher_out.reshape(GLOBALS, G_TOK, D), back_global.reshape(GLOBALS, G_TOK, D), back_local.reshape(LOCALS, L_TOK, D), new_student, new_teacher, new_first, new_second)
```

```python
import jax
import jax.numpy as jnp
from jax import lax
from jax.sharding import Mesh, PartitionSpec as P

HEADS = 12
HEAD_DIM = 64


norm_eps = 1e-06
beta_one = 0.9
beta_two = 0.999
corr_one = 1.0 - 0.9**10
corr_two = 1.0 - 0.999**10
learn_rate = 0.002
decay_rate = 0.04
momentum = 0.994
adam_eps = 1e-08


def attend(crops, weight):
    crop_count, length, feature = crops.shape
    inputs = crops.astype(jnp.float32)
    average = jnp.mean(inputs, axis=-1, keepdims=True)
    centred = inputs - average
    variance = jnp.mean(centred * centred, axis=-1, keepdims=True)
    normed = (centred * lax.rsqrt(variance + norm_eps)).astype(jnp.bfloat16)
    projected = jnp.dot(
        normed.reshape(crop_count * length, feature), weight, preferred_element_type=jnp.float32
    )
    projected = projected.astype(jnp.bfloat16).reshape(crop_count, length, 3, HEADS, HEAD_DIM)
    queries = projected[:, :, 0]
    key_rows = projected[:, :, 1]
    value_rows = projected[:, :, 2]
    scores = jnp.einsum(
        "nqhe,nkhe->nhqk", queries, key_rows, preferred_element_type=jnp.float32
    ) * HEAD_DIM ** (-0.5)
    exponent = jnp.exp(scores)
    probability = (exponent / jnp.sum(exponent, axis=-1, keepdims=True)).astype(jnp.bfloat16)
    heads_out = jnp.einsum(
        "nhqk,nkhe->nqhe", probability, value_rows, preferred_element_type=jnp.float32
    )
    return heads_out.reshape(crop_count, length, HEADS * HEAD_DIM)


def adam_update(weight, teacher, first, second, gradient):
    first = beta_one * first + (1.0 - beta_one) * gradient
    second = beta_two * second + (1.0 - beta_two) * gradient * gradient
    update = first / corr_one / (jnp.sqrt(second / corr_two) + adam_eps)
    weight_new = weight - learn_rate * (update + decay_rate * weight)
    teacher_new = momentum * teacher + (1.0 - momentum) * weight_new
    return (weight_new, teacher_new, first, second)


ROWS = 24
MAIN = 512
TAIL = 64
QUARTER = MAIN + TAIL
AXES = ("zh", "yh", "yl", "c", "zl", "x")
FSDP = ("zh", "yh", "yl", "c")
SWAP = [(0, 1), (1, 0)]


def own_quarter(half):
    place = lax.axis_index("x")
    main = lax.dynamic_slice_in_dim(half, place * MAIN, MAIN, axis=1)
    tail = lax.dynamic_slice_in_dim(half, 4 * MAIN + place * TAIL, TAIL, axis=1)
    return jnp.concatenate([main, tail], axis=1)


def join_quarters(parts):
    rows = parts.shape[1]
    main = parts[:, :, :MAIN].transpose(1, 0, 2).reshape(rows, 4 * MAIN)
    tail = parts[:, :, MAIN:].transpose(1, 0, 2).reshape(rows, 4 * TAIL)
    return jnp.concatenate([main, tail], axis=1)


def split_quarters(whole):
    rows = whole.shape[0]
    main = whole[:, : 4 * MAIN].reshape(rows, 4, MAIN).transpose(1, 0, 2)
    tail = whole[:, 4 * MAIN :].reshape(rows, 4, TAIL).transpose(1, 0, 2)
    return jnp.concatenate([main, tail], axis=2)


def gather_rows(half):
    part = own_quarter(half)
    column = lax.all_to_all(
        jnp.broadcast_to(part[None], (8, ROWS, QUARTER)), ("zh", "yh"), 0, 0, tiled=True
    )
    block = column.reshape(8 * ROWS, QUARTER)
    own = lax.all_to_all(
        jnp.broadcast_to(block[None], (8, 8 * ROWS, QUARTER)), ("x", "yl"), 0, 0, tiled=True
    ).reshape(4, 16 * ROWS, QUARTER)
    other = lax.ppermute(own, "c", SWAP)
    return own, other


def add_up(own, other):
    total = own.astype(jnp.float32) + lax.ppermute(other, "c", SWAP).astype(jnp.float32)
    total = total.astype(jnp.bfloat16).reshape(8, 8 * ROWS, QUARTER)
    shares = lax.all_to_all(total, ("x", "yl"), 0, 0, tiled=True)
    total = jnp.sum(shares.astype(jnp.float32), axis=0).astype(jnp.bfloat16)
    shares = lax.all_to_all(total.reshape(8, ROWS, QUARTER), ("zh", "yh"), 0, 0, tiled=True)
    total = jnp.sum(shares.astype(jnp.float32), axis=0).astype(jnp.bfloat16)
    shares = lax.all_to_all(
        jnp.broadcast_to(total[None], (16, ROWS, QUARTER)), ("zl", "x"), 0, 0, tiled=True
    )
    total = jnp.sum(shares.astype(jnp.float32).reshape(4, 4, ROWS, QUARTER), axis=0)
    return join_quarters(total)


def on_device(
    student_global,
    student_local,
    teacher_global,
    grad_global,
    grad_local,
    student_qkv,
    teacher_qkv,
    first_moment,
    second_moment,
):
    student_half = student_qkv.astype(jnp.bfloat16)
    teacher_half = teacher_qkv.astype(jnp.bfloat16)
    teacher_full = lax.all_gather(teacher_half, FSDP, axis=0, tiled=True)
    own, other = gather_rows(student_half)
    core = lax.axis_index("c")
    both = jnp.where(core == 0, jnp.stack([own, other]), jnp.stack([other, own]))
    both = both.reshape(2, 4, 2, 8, ROWS, QUARTER).transpose(1, 3, 2, 0, 4, 5)
    student_full = join_quarters(both.reshape(4, 32 * ROWS, QUARTER))

    def forward(global_in, local_in, weight_in):
        return (attend(global_in, weight_in), attend(local_in, weight_in))

    results, pullback = jax.vjp(forward, student_global, student_local, student_full)
    back_g, back_l, weight_term = pullback(
        (grad_global.astype(jnp.float32), grad_local.astype(jnp.float32))
    )
    teacher_rows = attend(teacher_global, teacher_full).astype(jnp.bfloat16)
    token_total = (
        (
            student_global.shape[0] * student_global.shape[1]
            + student_local.shape[0] * student_local.shape[1]
        )
        * lax.axis_size(AXES)
    )
    grad_scale = 1.0 / jnp.sqrt(jnp.float32(token_total))
    parts = split_quarters(weight_term).reshape(4, 8, 2, 2, ROWS, QUARTER)
    parts = parts.transpose(3, 0, 2, 1, 4, 5).reshape(2, 4, 16 * ROWS, QUARTER)
    gradient = add_up(parts[core], parts[1 - core]) * grad_scale
    new_student, new_teacher, new_first, new_second = adam_update(
        student_qkv, teacher_qkv, first_moment, second_moment, gradient
    )
    return (
        results[0].astype(jnp.bfloat16),
        results[1].astype(jnp.bfloat16),
        teacher_rows,
        back_g,
        back_l,
        new_student,
        new_teacher,
        new_first,
        new_second,
    )


def solution(mesh):
    mesh = Mesh(mesh.devices.reshape(2, 4, 2, 2, 4, 4), AXES)
    return jax.shard_map(
        on_device,
        mesh=mesh,
        in_specs=(
            P(AXES, None, None),
            P(AXES, None, None),
            P(AXES, None, None),
            P(AXES, None, None),
            P(AXES, None, None),
            P(FSDP, None),
            P(FSDP, None),
            P(FSDP, None),
            P(FSDP, None),
        ),
        out_specs=(
            P(AXES, None, None),
            P(AXES, None, None),
            P(AXES, None, None),
            P(AXES, None, None),
            P(AXES, None, None),
            P(FSDP, None),
            P(FSDP, None),
            P(FSDP, None),
            P(FSDP, None),
        ),
        check_vma=False,
    )
```

```python
import jax
import jax.numpy as jnp
from jax import lax
from jax.experimental import pallas as pl
from jax.experimental.pallas import tpu as pltpu
from jax.sharding import Mesh, PartitionSpec as P

HEADS = 12
D = 768
G_TOK = 257
LOCAL_AT = 272
L_ALL = 74
ROWS_S = 352
ROWS_T = 272
KEYS = 384
PAIRS = 6
MAIN = 512
TAIL = 64
QUARTER = MAIN + 2 * TAIL
HALF = 384
NT = (((1,), (1,)), ((), ()))
NN = (((1,), (0,)), ((), ()))
TN = (((0,), (0,)), ((), ()))
norm_eps = 1e-06


def dot(a, b, dims):
    return lax.dot_general(a, b, dims, preferred_element_type=jnp.float32)


def normalize(x):
    x = x.astype(jnp.float32)
    centred = x - jnp.mean(x, axis=-1, keepdims=True)
    scale = lax.rsqrt(jnp.mean(centred * centred, axis=-1, keepdims=True) + norm_eps)
    return centred * scale, scale


def one_hot(order_ref):
    row = lax.broadcasted_iota(jnp.int32, (D, D), 0)
    return jnp.where(row == order_ref[...], 1.0, 0.0).astype(jnp.bfloat16)


def project(n_ref, wo_ref, wx_ref, tail_ref, p_ref):
    own = n_ref[:, :HALF]
    other = n_ref[:, HALF:]
    for g in range(4):
        part = dot(own, wo_ref[g, :, :MAIN], NN) + dot(other, wx_ref[g, :, :MAIN], NN)
        p_ref[:, g * MAIN : (g + 1) * MAIN] = part.astype(jnp.bfloat16)
        tail_ref[:HALF, g * TAIL : (g + 1) * TAIL] = wo_ref[g, :, MAIN : MAIN + TAIL]
        tail_ref[HALF:, g * TAIL : (g + 1) * TAIL] = wx_ref[g, :, MAIN : MAIN + TAIL]
    part = dot(n_ref[...], tail_ref[...], NN)
    p_ref[:, 4 * MAIN :] = part.astype(jnp.bfloat16)


def doubled(x, first):
    rows = x.shape[0]
    zero = jnp.zeros_like(x)
    pad = jnp.zeros((KEYS - rows, 128), x.dtype)
    return jnp.concatenate([jnp.where(first, x, zero), pad, jnp.where(first, zero, x), pad], axis=0)


def bias_of(rows):
    q = lax.broadcasted_iota(jnp.int32, (rows, KEYS), 0)
    k = lax.broadcasted_iota(jnp.int32, (rows, KEYS), 1)
    in_global = (q < LOCAL_AT) & (k < G_TOK)
    in_local = (q >= LOCAL_AT) & (k >= LOCAL_AT) & (k < LOCAL_AT + L_ALL) & (q % 2 == k % 2)
    return jnp.where(in_global | in_local, 0.0, -1e30)


def softmax(scores, bias):
    e = jnp.exp(scores + bias)
    return e * (1.0 / jnp.sum(e, axis=-1, keepdims=True))


def pre_kernel(xg_ref, xl_ref, order_ref, n_ref, nt_ref, scr):
    scr[...] = jnp.zeros_like(scr)
    scr[:G_TOK, :] = normalize(xg_ref[...])[0].astype(jnp.bfloat16)
    scr[LOCAL_AT : LOCAL_AT + L_ALL, :] = normalize(xl_ref[...])[0].astype(jnp.bfloat16)
    n = dot(scr[...], one_hot(order_ref), NN)
    n_ref[...] = n.astype(jnp.bfloat16)
    nt_ref[...] = n.T.astype(jnp.bfloat16)


def student_kernel(
    n_ref, nt_ref, wo_ref, wx_ref, gg_ref, gl_ref,
    og_ref, ol_ref, dwo_ref, dwx_ref, dp_ref,
    p_scr, do_scr, tail_scr, bias_scr,
):
    do_scr[...] = jnp.zeros_like(do_scr)
    do_scr[:G_TOK, :] = gg_ref[...]
    do_scr[LOCAL_AT : LOCAL_AT + L_ALL, :] = gl_ref[...]
    bias_scr[...] = bias_of(ROWS_S)
    project(n_ref, wo_ref, wx_ref, tail_scr, p_scr)
    first = lax.broadcasted_iota(jnp.int32, (ROWS_S, 128), 1) < 64

    @pl.loop(0, PAIRS)
    def _(i):
        at = [pl.ds(pl.multiple_of(part * D + i * 128, 128), 128) for part in range(3)]
        q, k, v = (p_scr[:, a] for a in at)
        do = do_scr[:, at[0]]
        kd = doubled(k * jnp.bfloat16(0.125), first)
        vd = doubled(v, first)
        scores = dot(q, kd, NT)
        bias = bias_scr[...]
        p = [softmax(scores[:, h * KEYS : (h + 1) * KEYS], bias) for h in range(2)]
        pb = jnp.concatenate([x.astype(jnp.bfloat16) for x in p], axis=1)
        o = dot(pb, vd, NN)
        dv = dot(pb, do, TN)
        dprob = dot(do, vd, NT)
        od = o * do.astype(jnp.float32)
        delta = [
            jnp.sum(jnp.where(first if h == 0 else ~first, od, 0.0), axis=-1, keepdims=True)
            for h in range(2)
        ]
        ds = jnp.concatenate(
            [
                (p[h] * (dprob[:, h * KEYS : (h + 1) * KEYS] - delta[h])).astype(jnp.bfloat16)
                for h in range(2)
            ],
            axis=1,
        )
        dq = dot(ds, kd, NN)
        dk = dot(ds, q * jnp.bfloat16(0.125), TN)
        o = o.astype(jnp.bfloat16)
        og_ref[:, at[0]] = o[:G_TOK]
        ol_ref[:, at[0]] = o[LOCAL_AT : LOCAL_AT + L_ALL]
        dp_ref[:, at[0]] = dq.astype(jnp.bfloat16)
        dp_ref[:, at[1]] = jnp.where(first, dk[:ROWS_S], dk[KEYS : KEYS + ROWS_S]).astype(jnp.bfloat16)
        dp_ref[:, at[2]] = jnp.where(first, dv[:ROWS_S], dv[KEYS : KEYS + ROWS_S]).astype(jnp.bfloat16)

    for out_ref, rows in ((dwx_ref, slice(HALF, D)), (dwo_ref, slice(0, HALF))):
        nt = nt_ref[rows, :]
        for g in range(4):
            out_ref[g, :, :MAIN] = dot(nt, dp_ref[:, g * MAIN : (g + 1) * MAIN], NN).astype(jnp.bfloat16)
        tail = dot(nt, dp_ref[:, 4 * MAIN :], NN).astype(jnp.bfloat16)
        for g in range(4):
            out_ref[g, :, MAIN : MAIN + TAIL] = tail[:, g * TAIL : (g + 1) * TAIL]
            out_ref[g, :, MAIN + TAIL :] = jnp.zeros((HALF, TAIL), jnp.bfloat16)


def post_kernel(dp_ref, wo_ref, wx_ref, xg_ref, xl_ref, order_ref, bg_ref, bl_ref, tail_scr):
    halves = []
    for w_ref, at in ((wo_ref, 0), (wx_ref, HALF)):
        for g in range(4):
            tail_scr[at : at + HALF, g * TAIL : (g + 1) * TAIL] = w_ref[g, :, MAIN : MAIN + TAIL]
        total = dot(dp_ref[:, 4 * MAIN :], tail_scr[at : at + HALF, :], NT)
        for g in range(4):
            total += dot(dp_ref[:, g * MAIN : (g + 1) * MAIN], w_ref[g, :, :MAIN], NT)
        halves.append(total.astype(jnp.bfloat16))
    dn = dot(jnp.concatenate(halves, axis=1), one_hot(order_ref), NT)
    for x_ref, out_ref, at, count in ((xg_ref, bg_ref, 0, G_TOK), (xl_ref, bl_ref, LOCAL_AT, L_ALL)):
        hat, scale = normalize(x_ref[...])
        d = dn[at : at + count]
        mean = jnp.mean(d, axis=-1, keepdims=True)
        along = jnp.mean(d * hat, axis=-1, keepdims=True)
        out_ref[...] = (scale * (d - mean - hat * along)).astype(jnp.bfloat16)


def teacher_kernel(x_ref, order_ref, wo_ref, wx_ref, o_ref, n_scr, scr, p_scr, tail_scr, bias_scr):
    scr[...] = jnp.zeros_like(scr)
    scr[:G_TOK, :] = normalize(x_ref[...])[0].astype(jnp.bfloat16)
    n_scr[...] = dot(scr[...], one_hot(order_ref), NN).astype(jnp.bfloat16)
    bias_scr[...] = bias_of(ROWS_T)
    project(n_scr, wo_ref, wx_ref, tail_scr, p_scr)
    first = lax.broadcasted_iota(jnp.int32, (ROWS_T, 128), 1) < 64

    @pl.loop(0, PAIRS)
    def _(i):
        at = [pl.ds(pl.multiple_of(part * D + i * 128, 128), 128) for part in range(3)]
        q, k, v = (p_scr[:, a] for a in at)
        scores = dot(q, doubled(k * jnp.bfloat16(0.125), first), NT)
        bias = bias_scr[...]
        p = [softmax(scores[:, h * KEYS : (h + 1) * KEYS], bias).astype(jnp.bfloat16) for h in range(2)]
        o = dot(jnp.concatenate(p, axis=1), doubled(v, first), NN)
        o_ref[:, at[0]] = o[:G_TOK].astype(jnp.bfloat16)


BF = jnp.bfloat16
VMEM = pltpu.CompilerParams(vmem_limit_bytes=40 * 2**20)


def call(kernel, outs, scratch, flops, nbytes, *args):
    return pl.pallas_call(
        kernel,
        out_shape=[jax.ShapeDtypeStruct(s, BF) for s in outs],
        scratch_shapes=[pltpu.VMEM(s, t) for s, t in scratch],
        compiler_params=VMEM,
        cost_estimate=pl.CostEstimate(flops=flops, bytes_accessed=nbytes, transcendentals=0),
    )(*args)


def pre(xg, xl, order):
    return call(pre_kernel, [(ROWS_S, D), (D, ROWS_S)], [((ROWS_S, D), BF)], 10**9, 10**6, xg, xl, order)


def student(n, nt, wo, wx, gg, gl):
    return call(
        student_kernel,
        [(G_TOK, D), (L_ALL, D), (4, HALF, QUARTER), (4, HALF, QUARTER), (ROWS_S, 3 * D)],
        [((ROWS_S, 3 * D), BF), ((ROWS_S, D), BF), ((D, 256), BF), ((ROWS_S, KEYS), jnp.float32)],
        8 * 10**9, 10**7, n, nt, wo, wx, gg, gl,
    )


def post(dp, wo, wx, xg, xl, order):
    return call(post_kernel, [(G_TOK, D), (L_ALL, D)], [((D, 256), BF)], 3 * 10**9, 6 * 10**6, dp, wo, wx, xg, xl, order)


def teacher(x, order, wo, wx):
    return call(
        teacher_kernel,
        [(G_TOK, D)],
        [((ROWS_T, D), BF), ((ROWS_T, D), BF), ((ROWS_T, 3 * D), BF), ((D, 256), BF), ((ROWS_T, KEYS), jnp.float32)],
        3 * 10**9, 5 * 10**6, x, order, wo, wx,
    )[0]


ROWS = 24
AXES = ("zh", "yh", "yl", "c", "zl", "x")
FSDP = ("zh", "yh", "yl", "c")
SWAP = [(0, 1), (1, 0)]
TOKENS = 169472

beta_one = 0.9
beta_two = 0.999
corr_one = 1.0 - 0.9**10
corr_two = 1.0 - 0.999**10
learn_rate = 0.002
decay_rate = 0.04
momentum = 0.994
adam_eps = 1e-08


def adam_update(weight, teacher_weight, first, second, gradient):
    first = beta_one * first + (1.0 - beta_one) * gradient
    second = beta_two * second + (1.0 - beta_two) * gradient * gradient
    update = first / corr_one / (jnp.sqrt(second / corr_two) + adam_eps)
    weight_new = weight - learn_rate * (update + decay_rate * weight)
    teacher_new = momentum * teacher_weight + (1.0 - momentum) * weight_new
    return (weight_new, teacher_new, first, second)


def exchange(x, axes):
    return lax.all_to_all(x, axes, 0, 0, tiled=True)


def spread(x, count):
    return jnp.broadcast_to(x[None], (count,) + x.shape)


def swap(x):
    return lax.ppermute(x, "c", SWAP)


def own_quarter(half):
    place = lax.axis_index("x")
    main = lax.dynamic_slice_in_dim(half, place * MAIN, MAIN, axis=1)
    tail = lax.dynamic_slice_in_dim(half, 4 * MAIN + place * TAIL, TAIL, axis=1)
    return jnp.concatenate([main, tail, jnp.zeros_like(tail)], axis=1)


def join_quarters(parts):
    main = parts[:, :, :MAIN].transpose(1, 0, 2).reshape(ROWS, 4 * MAIN)
    tail = parts[:, :, MAIN : MAIN + TAIL].transpose(1, 0, 2).reshape(ROWS, 4 * TAIL)
    return jnp.concatenate([main, tail], axis=1)


def row_order():
    place = jnp.arange(D, dtype=jnp.int32)
    core = lax.axis_index("c").astype(jnp.int32)
    core = jnp.where(place < HALF, core, 1 - core)
    inner = place % HALF
    low, high, row = inner // 192, (inner % 192) // ROWS, inner % ROWS
    return (((high * 2 + low) * 2 + core) * ROWS + row)[None]


def add_up(own, other):
    total = own.astype(jnp.float32) + swap(other).astype(jnp.float32)
    total = total.astype(BF).reshape(8, 8 * ROWS, QUARTER)
    shares = exchange(total, ("x", "yl"))
    total = jnp.sum(shares.astype(jnp.float32), axis=0).astype(BF)
    shares = exchange(total.reshape(8, ROWS, QUARTER), ("zh", "yh"))
    total = jnp.sum(shares.astype(jnp.float32), axis=0).astype(BF)
    shares = exchange(spread(total, 16), ("zl", "x"))
    total = jnp.sum(shares.astype(jnp.float32).reshape(4, 4, ROWS, QUARTER), axis=0)
    return join_quarters(total)


def tokens(x):
    return x.transpose(1, 0, 2).reshape(L_ALL, D)


def crops(x):
    return x.reshape(L_ALL // 2, 2, D).transpose(1, 0, 2)


def on_device(
    student_global,
    student_local,
    teacher_global,
    grad_global,
    grad_local,
    student_qkv,
    teacher_qkv,
    first_moment,
    second_moment,
):
    order = row_order()
    parts = jnp.stack([own_quarter(student_qkv.astype(BF)), own_quarter(teacher_qkv.astype(BF))])
    columns = exchange(spread(parts, 8), ("zh", "yh"))
    columns = columns.transpose(1, 0, 2, 3).reshape(2, 8 * ROWS, QUARTER)
    student_own = exchange(spread(columns[0], 8), ("x", "yl")).reshape(4, HALF, QUARTER)
    student_other = swap(student_own)

    local = tokens(student_local)
    normed, normed_t = pre(student_global[0], local, order)
    out_g, out_l, own_term, other_term, d_projected = student(
        normed, normed_t, student_own, student_other, grad_global[0], tokens(grad_local)
    )
    teacher_own = exchange(spread(columns[1], 8), ("x", "yl")).reshape(4, HALF, QUARTER)
    teacher_other = swap(teacher_own)
    teacher_rows = teacher(teacher_global[0], order, teacher_own, teacher_other)
    back_g, back_l = post(d_projected, student_own, student_other, student_global[0], local, order)

    gradient = add_up(own_term, other_term) * (1.0 / jnp.sqrt(jnp.float32(TOKENS)))
    new_student, new_teacher, new_first, new_second = adam_update(
        student_qkv, teacher_qkv, first_moment, second_moment, gradient
    )
    return (
        out_g[None],
        crops(out_l),
        teacher_rows[None],
        back_g[None],
        crops(back_l),
        new_student,
        new_teacher,
        new_first,
        new_second,
    )


def solution(mesh):
    mesh = Mesh(mesh.devices.reshape(2, 4, 2, 2, 4, 4), AXES)
    crop, rows = P(AXES, None, None), P(FSDP, None)
    return jax.shard_map(
        on_device,
        mesh=mesh,
        in_specs=(crop,) * 5 + (rows,) * 4,
        out_specs=(crop,) * 5 + (rows,) * 4,
        check_vma=False,
    )
```

```python
import jax
import jax.numpy as jnp
from jax import lax
from jax.experimental import pallas as pl
from jax.experimental.pallas import tpu as pltpu
from jax.sharding import Mesh, PartitionSpec as P

HEADS = 12
D = 768
G_TOK = 257
LOCAL_AT = 272
L_ALL = 74
ROWS_S = 352
ROWS_T = 272
KEYS = 384
PAIRS = 6
MAIN = 512
SPAN = 192
BLOCK = 4 * SPAN + SPAN // 2
HALF = 384
NT = (((1,), (1,)), ((), ()))
NN = (((1,), (0,)), ((), ()))
TN = (((0,), (0,)), ((), ()))
norm_eps = 1e-06


def dot(a, b, dims):
    return lax.dot_general(a, b, dims, preferred_element_type=jnp.float32)


def normalize(x):
    x = x.astype(jnp.float32)
    centred = x - jnp.mean(x, axis=-1, keepdims=True)
    scale = lax.rsqrt(jnp.mean(centred * centred, axis=-1, keepdims=True) + norm_eps)
    return centred * scale, scale


def one_hot(order_ref):
    row = lax.broadcasted_iota(jnp.int32, (D, D), 0)
    return jnp.where(row == order_ref[...], 1.0, 0.0).astype(jnp.bfloat16)


def assemble(src, at, w_ref):
    for g in range(4):
        for low in range(2):
            block, top = 4 * low + g, at + low * SPAN
            for u in range(4):
                w_ref[top : top + SPAN, g * MAIN + u * 128 : g * MAIN + (u + 1) * 128] = src[
                    block, u * SPAN : (u + 1) * SPAN, :
                ]
            top, left = top + (g % 2) * (SPAN // 2), 4 * MAIN + (g // 2) * 128
            w_ref[top : top + SPAN // 2, left : left + 128] = src[block, 4 * SPAN :, :]


def project(n_ref, w_ref, p_ref):
    for part in range(3):
        at = slice(part * D, (part + 1) * D)
        p_ref[:, at] = dot(n_ref[...], w_ref[:, at], NN).astype(jnp.bfloat16)


def doubled(x, first):
    rows = x.shape[0]
    zero = jnp.zeros_like(x)
    pad = jnp.zeros((KEYS - rows, 128), x.dtype)
    return jnp.concatenate([jnp.where(first, x, zero), pad, jnp.where(first, zero, x), pad], axis=0)


def bias_of(rows):
    q = lax.broadcasted_iota(jnp.int32, (rows, KEYS), 0)
    k = lax.broadcasted_iota(jnp.int32, (rows, KEYS), 1)
    in_global = (q < LOCAL_AT) & (k < G_TOK)
    in_local = (q >= LOCAL_AT) & (k >= LOCAL_AT) & (k < LOCAL_AT + L_ALL) & (q % 2 == k % 2)
    return jnp.where(in_global | in_local, 0.0, -1e30)


def softmax(scores, bias):
    e = jnp.exp(scores + bias)
    return e * (1.0 / jnp.sum(e, axis=-1, keepdims=True))


def copies(pairs, sem):
    return [pltpu.make_async_copy(a, b, sem.at[i]) for i, (a, b) in enumerate(pairs)]


def start(moves):
    for move in moves:
        move.start()


def wait(moves):
    for move in moves:
        move.wait()


def cut_kernel(place_ref, sw_ref, tw_ref, out_ref):
    place = place_ref[0]
    main = pl.ds(pl.multiple_of(place * MAIN, MAIN), MAIN)
    tail = pl.ds(pl.multiple_of(4 * MAIN + place // 2 * 128, 128), 128)
    for i, ref in enumerate((sw_ref, tw_ref)):
        units = ref[:, main].astype(jnp.bfloat16)
        last = ref[:, tail].astype(jnp.bfloat16)
        for copy in range(8):
            for u in range(4):
                out_ref[copy, i, u] = units[:, u * 128 : (u + 1) * 128]
            out_ref[copy, i, 4] = last


def pre_kernel(xg_ref, xl_ref, order_ref, n_ref, nt_ref, scr):
    scr[...] = jnp.zeros_like(scr)
    scr[:G_TOK, :] = normalize(xg_ref[...])[0].astype(jnp.bfloat16)
    scr[LOCAL_AT : LOCAL_AT + L_ALL, :] = normalize(xl_ref[...])[0].astype(jnp.bfloat16)
    n = dot(scr[...], one_hot(order_ref), NN)
    n_ref[...] = n.astype(jnp.bfloat16)
    nt_ref[...] = n.T.astype(jnp.bfloat16)


def student_kernel(
    n_hbm, nt_hbm, gg_hbm, gl_hbm, wo_hbm, wx_hbm,
    og_hbm, ol_hbm, dwo_hbm, dwx_hbm, dp_hbm,
    n_ref, nt_ref, gg_ref, gl_ref, wo_ref, wx_ref, og_ref, ol_ref, dwo_ref, dwx_ref, dp_ref,
    p_scr, do_scr, w_scr, bias_scr, sem,
):
    pairs = [(wo_hbm, wo_ref), (wx_hbm, wx_ref), (n_hbm, n_ref)]
    pairs += [(gg_hbm, gg_ref), (gl_hbm, gl_ref), (nt_hbm, nt_ref)]
    loads = copies(pairs, sem)
    start(loads)
    bias_scr[...] = bias_of(ROWS_S)
    do_scr[...] = jnp.zeros_like(do_scr)
    loads[0].wait()
    assemble(wo_ref, 0, w_scr)
    loads[1].wait()
    assemble(wx_ref, HALF, w_scr)
    wait(loads[2:])
    do_scr[:G_TOK, :] = gg_ref[...]
    do_scr[LOCAL_AT : LOCAL_AT + L_ALL, :] = gl_ref[...]
    project(n_ref, w_scr, p_scr)
    first = lax.broadcasted_iota(jnp.int32, (ROWS_S, 128), 1) < 64

    @pl.loop(0, PAIRS)
    def _(i):
        at = [pl.ds(pl.multiple_of(part * D + i * 128, 128), 128) for part in range(3)]
        q, k, v = (p_scr[:, a] for a in at)
        do = do_scr[:, at[0]]
        kd = doubled(k * jnp.bfloat16(0.125), first)
        vd = doubled(v, first)
        scores = dot(q, kd, NT)
        bias = bias_scr[...]
        p = [softmax(scores[:, h * KEYS : (h + 1) * KEYS], bias) for h in range(2)]
        pb = jnp.concatenate([x.astype(jnp.bfloat16) for x in p], axis=1)
        o = dot(pb, vd, NN)
        dv = dot(pb, do, TN)
        dprob = dot(do, vd, NT)
        od = o * do.astype(jnp.float32)
        delta = [
            jnp.sum(jnp.where(first if h == 0 else ~first, od, 0.0), axis=-1, keepdims=True)
            for h in range(2)
        ]
        ds = jnp.concatenate(
            [
                (p[h] * (dprob[:, h * KEYS : (h + 1) * KEYS] - delta[h])).astype(jnp.bfloat16)
                for h in range(2)
            ],
            axis=1,
        )
        dq = dot(ds, kd, NN)
        dk = dot(ds, q * jnp.bfloat16(0.125), TN)
        o = o.astype(jnp.bfloat16)
        og_ref[:, at[0]] = o[:G_TOK]
        ol_ref[:, at[0]] = o[LOCAL_AT : LOCAL_AT + L_ALL]
        dp_ref[:, at[0]] = dq.astype(jnp.bfloat16)
        dp_ref[:, at[1]] = jnp.where(first, dk[:ROWS_S], dk[KEYS : KEYS + ROWS_S]).astype(jnp.bfloat16)
        dp_ref[:, at[2]] = jnp.where(first, dv[:ROWS_S], dv[KEYS : KEYS + ROWS_S]).astype(jnp.bfloat16)

    pairs = [(og_ref, og_hbm), (ol_ref, ol_hbm), (dp_ref, dp_hbm), (dwx_ref, dwx_hbm), (dwo_ref, dwo_hbm)]
    stores = copies(pairs, sem)
    start(stores[:3])
    for out_ref, rows, move in ((dwx_ref, slice(HALF, D), stores[3]), (dwo_ref, slice(0, HALF), stores[4])):
        nt = nt_ref[rows, :]
        for g in range(4):
            term = dot(nt, dp_ref[:, g * MAIN : (g + 1) * MAIN], NN).astype(jnp.bfloat16)
            for low in range(2):
                for u in range(4):
                    out_ref[4 * low + g, u * SPAN : (u + 1) * SPAN, :] = term[
                        low * SPAN : (low + 1) * SPAN, u * 128 : (u + 1) * 128
                    ]
        term = dot(nt, dp_ref[:, 4 * MAIN :], NN).astype(jnp.bfloat16)
        for g in range(4):
            for low in range(2):
                top, left = low * SPAN + (g % 2) * (SPAN // 2), (g // 2) * 128
                out_ref[4 * low + g, 4 * SPAN :, :] = term[top : top + SPAN // 2, left : left + 128]
        move.start()
    wait(stores)


def post_kernel(
    dp_hbm, xg_hbm, xl_hbm, wo_ref, wx_ref, order_ref, bg_hbm, bl_hbm,
    dp_ref, xg_ref, xl_ref, bg_ref, bl_ref, w_scr, sem,
):
    loads = copies([(dp_hbm, dp_ref), (xg_hbm, xg_ref), (xl_hbm, xl_ref)], sem)
    start(loads)
    assemble(wo_ref, 0, w_scr)
    assemble(wx_ref, HALF, w_scr)
    wait(loads)
    dn = dot(dp_ref[...], w_scr[...], NT).astype(jnp.bfloat16)
    dn = dot(dn, one_hot(order_ref), NT)
    for x_ref, out_ref, at, count in ((xg_ref, bg_ref, 0, G_TOK), (xl_ref, bl_ref, LOCAL_AT, L_ALL)):
        hat, scale = normalize(x_ref[...])
        d = dn[at : at + count]
        mean = jnp.mean(d, axis=-1, keepdims=True)
        along = jnp.mean(d * hat, axis=-1, keepdims=True)
        out_ref[...] = (scale * (d - mean - hat * along)).astype(jnp.bfloat16)
    stores = copies([(bg_ref, bg_hbm), (bl_ref, bl_hbm)], sem)
    start(stores)
    wait(stores)


def teacher_kernel(x_hbm, order_ref, wo_ref, wx_ref, o_ref, x_ref, n_scr, scr, p_scr, w_scr, bias_scr, sem):
    loads = copies([(x_hbm, x_ref)], sem)
    start(loads)
    assemble(wo_ref, 0, w_scr)
    assemble(wx_ref, HALF, w_scr)
    bias_scr[...] = bias_of(ROWS_T)
    scr[...] = jnp.zeros_like(scr)
    wait(loads)
    scr[:G_TOK, :] = normalize(x_ref[...])[0].astype(jnp.bfloat16)
    n_scr[...] = dot(scr[...], one_hot(order_ref), NN).astype(jnp.bfloat16)
    project(n_scr, w_scr, p_scr)
    first = lax.broadcasted_iota(jnp.int32, (ROWS_T, 128), 1) < 64

    @pl.loop(0, PAIRS)
    def _(i):
        at = [pl.ds(pl.multiple_of(part * D + i * 128, 128), 128) for part in range(3)]
        q, k, v = (p_scr[:, a] for a in at)
        scores = dot(q, doubled(k * jnp.bfloat16(0.125), first), NT)
        bias = bias_scr[...]
        p = [softmax(scores[:, h * KEYS : (h + 1) * KEYS], bias).astype(jnp.bfloat16) for h in range(2)]
        o = dot(jnp.concatenate(p, axis=1), doubled(v, first), NN)
        o_ref[:, at[0]] = o[:G_TOK].astype(jnp.bfloat16)


BF = jnp.bfloat16


HBM = pl.BlockSpec(memory_space=pltpu.HBM)
HERE = pl.BlockSpec(memory_space=pltpu.VMEM)
F32 = jnp.float32


def call(kernel, mib, ins, outs, scratch, sems, flops, nbytes, *args):
    scratch = [pltpu.VMEM(s, t) for s, t in scratch]
    return pl.pallas_call(
        kernel,
        in_specs=ins,
        out_specs=[spec for _, spec in outs],
        out_shape=[jax.ShapeDtypeStruct(s, BF) for s, _ in outs],
        scratch_shapes=scratch + [pltpu.SemaphoreType.DMA((n,)) for n in sems],
        compiler_params=pltpu.CompilerParams(vmem_limit_bytes=mib * 2**20),
        cost_estimate=pl.CostEstimate(flops=flops, bytes_accessed=nbytes, transcendentals=0),
    )(*args)


def cut(place, sw, tw):
    ins = [pl.BlockSpec(memory_space=pltpu.SMEM), HERE, HERE]
    return call(cut_kernel, 12, ins, [((8, 2, 5, 24, 128), HERE)], [], [], 10**6, 10**6, place, sw, tw)[0]


def pre(xg, xl, order):
    outs = [((ROWS_S, D), HERE), ((D, ROWS_S), HERE)]
    return call(pre_kernel, 12, [HERE] * 3, outs, [((ROWS_S, D), BF)], [], 10**9, 10**6, xg, xl, order)


def student(n, nt, wo, wx, gg, gl):
    block = (8, BLOCK, 128)
    outs = [(G_TOK, D), (L_ALL, D), block, block, (ROWS_S, 3 * D)]
    here = [(ROWS_S, D), (D, ROWS_S), (G_TOK, D), (L_ALL, D), block, block] + outs
    here += [(ROWS_S, 3 * D), (ROWS_S, D), (D, 3 * D)]
    return call(
        student_kernel, 56, [HBM] * 6, [(s, HBM) for s in outs],
        [(s, BF) for s in here] + [((ROWS_S, KEYS), F32)], [6],
        8 * 10**9, 10**7, n, nt, gg, gl, wo, wx,
    )


def add_kernel(a_ref, b_ref, out_ref):
    out_ref[...] = (a_ref[...].astype(F32) + b_ref[...].astype(F32)).astype(BF)


def add(a, b):
    spec = pl.BlockSpec((2, BLOCK, 128), lambda i: (i, 0, 0))
    return pl.pallas_call(
        add_kernel,
        grid=(4,),
        in_specs=[spec, spec],
        out_specs=spec,
        out_shape=jax.ShapeDtypeStruct((8, BLOCK, 128), BF),
        compiler_params=pltpu.CompilerParams(vmem_limit_bytes=56 * 2**20),
        cost_estimate=pl.CostEstimate(flops=10**6, bytes_accessed=5 * 10**6, transcendentals=0),
    )(a, b)


def post(dp, wo, wx, xg, xl, order):
    outs = [((G_TOK, D), HBM), ((L_ALL, D), HBM)]
    here = [((ROWS_S, 3 * D), BF)] + [((G_TOK, D), BF), ((L_ALL, D), BF)] * 2 + [((D, 3 * D), BF)]
    return call(
        post_kernel, 20, [HBM] * 3 + [HERE] * 3, outs, here, [3],
        3 * 10**9, 6 * 10**6, dp, xg, xl, wo, wx, order,
    )


def teacher(x, order, wo, wx):
    here = [((G_TOK, D), BF), ((ROWS_T, D), BF), ((ROWS_T, D), BF), ((ROWS_T, 3 * D), BF)]
    here += [((D, 3 * D), BF), ((ROWS_T, KEYS), F32)]
    return call(
        teacher_kernel, 20, [HBM] + [HERE] * 3, [((G_TOK, D), HERE)], here, [1],
        3 * 10**9, 5 * 10**6, x, order, wo, wx,
    )[0]


ROWS = 24
AXES = ("zh", "yh", "yl", "c", "zl", "x")
FSDP = ("zh", "yh", "yl", "c")
SWAP = [(0, 1), (1, 0)]
TOKENS = 169472

beta_one = 0.9
beta_two = 0.999
corr_one = 1.0 - 0.9**10
corr_two = 1.0 - 0.999**10
learn_rate = 0.002
decay_rate = 0.04
momentum = 0.994
adam_eps = 1e-08


def adam_update(weight, teacher_weight, first, second, gradient):
    first = beta_one * first + (1.0 - beta_one) * gradient
    second = beta_two * second + (1.0 - beta_two) * gradient * gradient
    update = first / corr_one / (jnp.sqrt(second / corr_two) + adam_eps)
    weight_new = weight - learn_rate * (update + decay_rate * weight)
    teacher_new = momentum * teacher_weight + (1.0 - momentum) * weight_new
    return (weight_new, teacher_new, first, second)


def exchange(x, axes):
    return lax.all_to_all(x, axes, 0, 0, tiled=True)


def spread(x, count):
    return jnp.broadcast_to(x[None], (count,) + x.shape)


def swap(x):
    return lax.ppermute(x, "c", SWAP)


def gather_block(column):
    main = column[:, :4].transpose(1, 0, 2, 3).reshape(4 * SPAN, 128)
    tail = lax.dynamic_slice_in_dim(column[:, 4], lax.axis_index("x") % 2 * 4, 4, axis=0)
    return jnp.concatenate([main, tail.reshape(SPAN // 2, 128)], axis=0)


def by_row(block):
    main = block[: 4 * SPAN].reshape(4, 8, ROWS, 128).transpose(1, 0, 2, 3)
    tail = block[4 * SPAN :].reshape(4, 1, ROWS, 128)
    zero = jnp.zeros_like(tail)
    low = lax.axis_index("x") % 2 == 0
    tail = jnp.concatenate([jnp.where(low, tail, zero), jnp.where(low, zero, tail)], axis=0)
    return jnp.concatenate([main, tail], axis=1)


def join_units(units):
    main = units[:, :4].reshape(16, ROWS, 128)
    tail = units[:, 4].reshape(2, 2, ROWS, 128).sum(axis=1)
    whole = jnp.concatenate([main, tail], axis=0)
    return whole.transpose(1, 0, 2).reshape(ROWS, 3 * D)


def row_order():
    place = jnp.arange(D, dtype=jnp.int32)
    core = lax.axis_index("c").astype(jnp.int32)
    core = jnp.where(place < HALF, core, 1 - core)
    inner = place % HALF
    low, y_high, z_high, row = inner // SPAN, inner % SPAN // 48, inner % 48 // ROWS, inner % ROWS
    return ((((z_high * 4 + y_high) * 2 + low) * 2 + core) * ROWS + row)[None]


def add_up(own, other, beside):
    shares = exchange(add(own, swap(other)), ("yl", "x"))
    shares, beside = lax.optimization_barrier((shares, beside))
    total = jnp.sum(shares.astype(jnp.float32), axis=0).astype(BF)
    shares = exchange(by_row(total), ("yh", "zh"))
    total = jnp.sum(shares.astype(jnp.float32), axis=0).astype(BF)
    shares = exchange(spread(total, 16), ("x", "zl"))
    total = jnp.sum(shares.astype(jnp.float32).reshape(4, 4, 5, ROWS, 128), axis=1)
    return join_units(total), beside


def tokens(x):
    return x.transpose(1, 0, 2).reshape(L_ALL, D)


def crops(x):
    return x.reshape(L_ALL // 2, 2, D).transpose(1, 0, 2)


def on_device(
    student_global,
    student_local,
    teacher_global,
    grad_global,
    grad_local,
    student_qkv,
    teacher_qkv,
    first_moment,
    second_moment,
):
    order = row_order()
    place = lax.axis_index("x").astype(jnp.int32)[None]
    columns = exchange(cut(place, student_qkv, teacher_qkv), ("yh", "zh"))
    local, grad_rows = tokens(student_local), tokens(grad_local)
    normed, normed_t = pre(student_global[0], local, order)
    columns, normed, normed_t, local, grad_rows = lax.optimization_barrier(
        (columns, normed, normed_t, local, grad_rows)
    )
    student_own = exchange(spread(gather_block(columns[:, 0]), 8), ("yl", "x"))
    student_other = swap(student_own)
    out_g, out_l, own_term, other_term, d_projected = student(
        normed, normed_t, student_own, student_other, grad_global[0], grad_rows
    )
    teacher_own = exchange(spread(gather_block(columns[:, 1]), 8), ("yl", "x"))
    teacher_other = swap(teacher_own)
    teacher_rows = teacher(teacher_global[0], order, teacher_own, teacher_other)
    back_g, back_l = post(d_projected, student_own, student_other, student_global[0], local, order)

    gradient, (back_g, back_l) = add_up(own_term, other_term, (back_g, back_l))
    gradient = gradient * (1.0 / jnp.sqrt(jnp.float32(TOKENS)))
    new_student, new_teacher, new_first, new_second = adam_update(
        student_qkv, teacher_qkv, first_moment, second_moment, gradient
    )
    return (
        out_g[None],
        crops(out_l),
        teacher_rows[None],
        back_g[None],
        crops(back_l),
        new_student,
        new_teacher,
        new_first,
        new_second,
    )


def solution(mesh):
    mesh = Mesh(mesh.devices.reshape(2, 4, 2, 2, 4, 4), AXES)
    crop, rows = P(AXES, None, None), P(FSDP, None)
    return jax.shard_map(
        on_device,
        mesh=mesh,
        in_specs=(crop,) * 5 + (rows,) * 4,
        out_specs=(crop,) * 5 + (rows,) * 4,
        check_vma=False,
    )
```

```python
import jax
import jax.numpy as jnp
from jax import lax
from jax.experimental import pallas as pl
from jax.experimental.pallas import tpu as pltpu
from jax.sharding import Mesh, PartitionSpec as P

HEADS = 12
D = 768
G_TOK = 257
LOCAL_AT = 272
L_ALL = 74
ROWS_S = 352
ROWS_T = 272
KEYS = 384
PAIRS = 6
MAIN = 512
SPAN = 192
BLOCK = 4 * SPAN + SPAN // 2
HALF = 384
AT_N, AT_DO, AT_NT, AT_DP, AT_OL, SHELF = 0, 352, 704, 1472, 2528, 16384
NT = (((1,), (1,)), ((), ()))
NN = (((1,), (0,)), ((), ()))
TN = (((0,), (0,)), ((), ()))
norm_eps = 1e-06
BF = jnp.bfloat16
F32 = jnp.float32


def dot(a, b, dims):
    return lax.dot_general(a, b, dims, preferred_element_type=jnp.float32)


def normalize(x):
    x = x.astype(jnp.float32)
    centred = x - jnp.mean(x, axis=-1, keepdims=True)
    scale = lax.rsqrt(jnp.mean(centred * centred, axis=-1, keepdims=True) + norm_eps)
    return centred * scale, scale


def one_hot(order_ref):
    row = lax.broadcasted_iota(jnp.int32, (D, D), 0)
    return jnp.where(row == order_ref[...], 1.0, 0.0).astype(jnp.bfloat16)


def assemble(src, at, w_ref):
    for g in range(4):
        for low in range(2):
            block, top = 4 * low + g, at + low * SPAN
            for u in range(4):
                w_ref[top : top + SPAN, g * MAIN + u * 128 : g * MAIN + (u + 1) * 128] = src[
                    block, u * SPAN : (u + 1) * SPAN, :
                ]
            top, left = top + (g % 2) * (SPAN // 2), 4 * MAIN + (g // 2) * 128
            w_ref[top : top + SPAN // 2, left : left + 128] = src[block, 4 * SPAN :, :]


def project(n_ref, w_ref, p_ref):
    for part in range(3):
        at = slice(part * D, (part + 1) * D)
        p_ref[:, at] = dot(n_ref[...], w_ref[:, at], NN).astype(jnp.bfloat16)


def doubled(x, first):
    rows = x.shape[0]
    zero = jnp.zeros_like(x)
    pad = jnp.zeros((KEYS - rows, 128), x.dtype)
    return jnp.concatenate([jnp.where(first, x, zero), pad, jnp.where(first, zero, x), pad], axis=0)


def bias_of(shape, keys):
    q = lax.broadcasted_iota(jnp.int32, shape, 1 - keys)
    k = lax.broadcasted_iota(jnp.int32, shape, keys)
    in_global = (q < LOCAL_AT) & (k < G_TOK)
    in_local = (q >= LOCAL_AT) & (k >= LOCAL_AT) & (k < LOCAL_AT + L_ALL) & (q % 2 == k % 2)
    return jnp.where(in_global | in_local, 0.0, -1e30)


def softmax(scores, bias, keys):
    e = jnp.exp(scores + bias)
    return e * (1.0 / jnp.sum(e, axis=keys, keepdims=True))


def copies(pairs, sem):
    return [pltpu.make_async_copy(a, b, sem.at[i]) for i, (a, b) in enumerate(pairs)]


def start(moves):
    for move in moves:
        move.start()


def wait(moves):
    for move in moves:
        move.wait()


def cut_kernel(place_ref, sw_ref, tw_ref, out_ref):
    place = place_ref[0]
    main = pl.ds(pl.multiple_of(place * MAIN, MAIN), MAIN)
    tail = pl.ds(pl.multiple_of(4 * MAIN + place // 2 * 128, 128), 128)
    for i, ref in enumerate((sw_ref, tw_ref)):
        units = ref[:, main].astype(jnp.bfloat16)
        last = ref[:, tail].astype(jnp.bfloat16)
        for copy in range(8):
            for u in range(4):
                out_ref[copy, i, u] = units[:, u * 128 : (u + 1) * 128]
            out_ref[copy, i, 4] = last


def pre_kernel(xg_ref, xl_ref, gg_ref, gl_ref, order_ref, shelf, scr, n_ref, nt_ref, do_ref, sem):
    do_ref[...] = jnp.zeros_like(do_ref)
    do_ref[:G_TOK, :] = gg_ref[...]
    do_ref[LOCAL_AT : LOCAL_AT + L_ALL, :] = gl_ref[...]
    scr[...] = jnp.zeros_like(scr)
    scr[:G_TOK, :] = normalize(xg_ref[...])[0].astype(BF)
    scr[LOCAL_AT : LOCAL_AT + L_ALL, :] = normalize(xl_ref[...])[0].astype(BF)
    n = dot(scr[...], one_hot(order_ref), NN)
    n_ref[...] = n.astype(BF)
    nt_ref[...] = jnp.zeros_like(nt_ref)
    nt_ref[:, :ROWS_S] = n.T.astype(BF)
    moves = copies(
        [
            (n_ref, shelf.at[pl.ds(AT_N, ROWS_S), :]),
            (do_ref, shelf.at[pl.ds(AT_DO, ROWS_S), :]),
            (nt_ref, shelf.at[pl.ds(AT_NT, D), pl.ds(0, KEYS)]),
        ],
        sem,
    )
    start(moves)
    wait(moves)


def student_kernel(
    shelf_in, wo_ref, wx_ref,
    shelf, og_hbm, dwo_ref, dwx_ref,
    n_ref, do_scr, nt_ref, og_ref, ol_ref, dp_ref,
    p_scr, w_scr, bias_scr, sem,
):
    loads = copies(
        [
            (shelf_in.at[pl.ds(AT_N, ROWS_S), :], n_ref),
            (shelf_in.at[pl.ds(AT_DO, ROWS_S), :], do_scr),
            (shelf_in.at[pl.ds(AT_NT, D), pl.ds(0, KEYS)], nt_ref),
        ],
        sem,
    )
    start(loads)
    bias_scr[...] = bias_of((KEYS, ROWS_S), 0)
    ol_ref[...] = jnp.zeros_like(ol_ref)
    assemble(wo_ref, 0, w_scr)
    assemble(wx_ref, HALF, w_scr)
    wait(loads)
    project(n_ref, w_scr, p_scr)
    first = lax.broadcasted_iota(jnp.int32, (ROWS_S, 128), 1) < 64

    @pl.loop(0, PAIRS, unroll=PAIRS)
    def _(i):
        at = [pl.ds(pl.multiple_of(part * D + i * 128, 128), 128) for part in range(3)]
        q, k, v = (p_scr[:, a] for a in at)
        do = do_scr[:, at[0]]
        kd = doubled(k * jnp.bfloat16(0.125), first)
        vd = doubled(v, first)
        scores = dot(kd, q, NT)
        dprob = dot(vd, do, NT)
        bias = bias_scr[...]
        p, ds = [], []
        for h in range(2):
            at_h = slice(h * KEYS, (h + 1) * KEYS)
            prob = softmax(scores[at_h], bias, 0)
            both = prob * dprob[at_h]
            p.append(prob.astype(BF))
            ds.append((both - prob * jnp.sum(both, axis=0, keepdims=True)).astype(BF))
        p = jnp.concatenate(p, axis=0)
        ds = jnp.concatenate(ds, axis=0)
        dv = dot(p, do, NN)
        dk = dot(ds, q * jnp.bfloat16(0.125), NN)
        o = dot(p, vd, TN)
        dq = dot(ds, kd, TN)
        o = o.astype(jnp.bfloat16)
        og_ref[:, at[0]] = o[:G_TOK]
        ol_ref[:L_ALL, at[0]] = o[LOCAL_AT : LOCAL_AT + L_ALL]
        dp_ref[:, at[0]] = dq.astype(jnp.bfloat16)
        dp_ref[:, at[1]] = jnp.where(first, dk[:ROWS_S], dk[KEYS : KEYS + ROWS_S]).astype(jnp.bfloat16)
        dp_ref[:, at[2]] = jnp.where(first, dv[:ROWS_S], dv[KEYS : KEYS + ROWS_S]).astype(jnp.bfloat16)

    pairs = [(og_ref, og_hbm), (ol_ref, shelf.at[pl.ds(AT_OL, 80), :])]
    pairs += [
        (dp_ref.at[:, pl.ds(i * D, D)], shelf.at[pl.ds(AT_DP + i * ROWS_S, ROWS_S), :]) for i in range(3)
    ]
    stores = copies(pairs, sem)
    start(stores)
    for out_ref, rows in ((dwx_ref, slice(HALF, D)), (dwo_ref, slice(0, HALF))):
        nt = nt_ref[rows, :ROWS_S]
        for g in range(4):
            term = dot(nt, dp_ref[:, g * MAIN : (g + 1) * MAIN], NN).astype(jnp.bfloat16)
            for low in range(2):
                for u in range(4):
                    out_ref[4 * low + g, u * SPAN : (u + 1) * SPAN, :] = term[
                        low * SPAN : (low + 1) * SPAN, u * 128 : (u + 1) * 128
                    ]
        term = dot(nt, dp_ref[:, 4 * MAIN :], NN).astype(jnp.bfloat16)
        for g in range(4):
            for low in range(2):
                top, left = low * SPAN + (g % 2) * (SPAN // 2), (g // 2) * 128
                out_ref[4 * low + g, 4 * SPAN :, :] = term[top : top + SPAN // 2, left : left + 128]
    wait(stores)


def post_kernel(
    shelf, xg_hbm, xl_hbm, wo_ref, wx_ref, order_ref, bg_hbm, bl_hbm,
    dp_ref, xg_ref, xl_ref, bg_ref, bl_ref, w_scr, sem,
):
    pairs = [
        (shelf.at[pl.ds(AT_DP + i * ROWS_S, ROWS_S), :], dp_ref.at[:, pl.ds(i * D, D)]) for i in range(3)
    ]
    loads = copies(pairs + [(xg_hbm, xg_ref), (xl_hbm, xl_ref)], sem)
    start(loads)
    assemble(wo_ref, 0, w_scr)
    assemble(wx_ref, HALF, w_scr)
    wait(loads)
    dn = dot(dp_ref[...], w_scr[...], NT).astype(jnp.bfloat16)
    dn = dot(dn, one_hot(order_ref), NT)
    for x_ref, out_ref, at, count in ((xg_ref, bg_ref, 0, G_TOK), (xl_ref, bl_ref, LOCAL_AT, L_ALL)):
        hat, scale = normalize(x_ref[...])
        d = dn[at : at + count]
        mean = jnp.mean(d, axis=-1, keepdims=True)
        along = jnp.mean(d * hat, axis=-1, keepdims=True)
        out_ref[...] = (scale * (d - mean - hat * along)).astype(jnp.bfloat16)
    stores = copies([(bg_ref, bg_hbm), (bl_ref, bl_hbm)], sem)
    start(stores)
    wait(stores)


def teacher_kernel(x_hbm, order_ref, wo_ref, wx_ref, o_ref, x_ref, n_scr, scr, p_scr, w_scr, bias_scr, sem):
    loads = copies([(x_hbm, x_ref)], sem)
    start(loads)
    assemble(wo_ref, 0, w_scr)
    assemble(wx_ref, HALF, w_scr)
    bias_scr[...] = bias_of((ROWS_T, KEYS), 1)
    scr[...] = jnp.zeros_like(scr)
    wait(loads)
    scr[:G_TOK, :] = normalize(x_ref[...])[0].astype(jnp.bfloat16)
    n_scr[...] = dot(scr[...], one_hot(order_ref), NN).astype(jnp.bfloat16)
    project(n_scr, w_scr, p_scr)
    first = lax.broadcasted_iota(jnp.int32, (ROWS_T, 128), 1) < 64

    @pl.loop(0, PAIRS, unroll=PAIRS)
    def _(i):
        at = [pl.ds(pl.multiple_of(part * D + i * 128, 128), 128) for part in range(3)]
        q, k, v = (p_scr[:, a] for a in at)
        scores = dot(q, doubled(k * jnp.bfloat16(0.125), first), NT)
        bias = bias_scr[...]
        p = [softmax(scores[:, h * KEYS : (h + 1) * KEYS], bias, 1).astype(jnp.bfloat16) for h in range(2)]
        o = dot(jnp.concatenate(p, axis=1), doubled(v, first), NN)
        o_ref[:, at[0]] = o[:G_TOK].astype(jnp.bfloat16)


HBM = pl.BlockSpec(memory_space=pltpu.HBM)
HERE = pl.BlockSpec(memory_space=pltpu.VMEM)


def call(kernel, mib, ins, outs, scratch, sems, flops, nbytes, *args, aliases=None):
    scratch = [pltpu.VMEM(s, t) for s, t in scratch]
    return pl.pallas_call(
        kernel,
        in_specs=ins,
        out_specs=[spec for _, spec in outs],
        out_shape=[jax.ShapeDtypeStruct(s, BF) for s, _ in outs],
        scratch_shapes=scratch + [pltpu.SemaphoreType.DMA((n,)) for n in sems],
        input_output_aliases=aliases or {},
        compiler_params=pltpu.CompilerParams(vmem_limit_bytes=mib * 2**20),
        cost_estimate=pl.CostEstimate(flops=flops, bytes_accessed=nbytes, transcendentals=0),
    )(*args)


def cut(place, sw, tw):
    ins = [pl.BlockSpec(memory_space=pltpu.SMEM), HERE, HERE]
    return call(cut_kernel, 56, ins, [((8, 2, 5, 24, 128), HERE)], [], [], 10**6, 10**6, place, sw, tw)[0]


SHELF_SHAPE = (SHELF, D)


def pre(xg, xl, gg, gl, order):
    here = [((ROWS_S, D), BF), ((ROWS_S, D), BF), ((D, KEYS), BF), ((ROWS_S, D), BF)]
    return call(
        pre_kernel, 44, [HERE] * 5, [(SHELF_SHAPE, HBM)], here, [3],
        10**9, 10**6, xg, xl, gg, gl, order,
    )[0]


def student(shelf, wo, wx):
    block = (8, BLOCK, 128)
    outs = [(SHELF_SHAPE, HBM), ((G_TOK, D), HBM), (block, HERE), (block, HERE)]
    here = [(ROWS_S, D), (ROWS_S, D), (D, KEYS), (G_TOK, D), (80, D)]
    here += [(ROWS_S, 3 * D), (ROWS_S, 3 * D), (D, 3 * D)]
    return call(
        student_kernel, 42, [HBM, HERE, HERE], outs, [(s, BF) for s in here] + [((KEYS, ROWS_S), F32)], [5],
        8 * 10**9, 10**7, shelf, wo, wx, aliases={0: 0},
    )


def post(shelf, wo, wx, xg, xl, order):
    outs = [((G_TOK, D), HBM), ((L_ALL, D), HBM)]
    here = [((ROWS_S, 3 * D), BF)] + [((G_TOK, D), BF), ((L_ALL, D), BF)] * 2 + [((D, 3 * D), BF)]
    return call(
        post_kernel, 42, [HBM] * 3 + [HERE] * 3, outs, here, [5],
        3 * 10**9, 6 * 10**6, shelf, xg, xl, wo, wx, order,
    )


def teacher(x, order, wo, wx):
    here = [((G_TOK, D), BF), ((ROWS_T, D), BF), ((ROWS_T, D), BF), ((ROWS_T, 3 * D), BF)]
    here += [((D, 3 * D), BF), ((ROWS_T, KEYS), F32)]
    return call(
        teacher_kernel, 20, [HBM] + [HERE] * 3, [((G_TOK, D), HERE)], here, [1],
        3 * 10**9, 5 * 10**6, x, order, wo, wx,
    )[0]


ROWS = 24
AXES = ("zh", "yh", "yl", "c", "zlh", "zll", "x")
FSDP = ("zh", "yh", "yl", "c")
SWAP = [(0, 1), (1, 0)]
TOKENS = 169472

beta_one = 0.9
beta_two = 0.999
corr_one = 1.0 - 0.9**10
corr_two = 1.0 - 0.999**10
learn_rate = 0.002
decay_rate = 0.04
momentum = 0.994
adam_eps = 1e-08


def adam_update(weight, teacher_weight, first, second, gradient):
    first = beta_one * first + (1.0 - beta_one) * gradient
    second = beta_two * second + (1.0 - beta_two) * gradient * gradient
    update = first / corr_one / (jnp.sqrt(second / corr_two) + adam_eps)
    weight_new = weight - learn_rate * (update + decay_rate * weight)
    teacher_new = momentum * teacher_weight + (1.0 - momentum) * weight_new
    return (weight_new, teacher_new, first, second)


def exchange(x, axes):
    return lax.all_to_all(x, axes, 0, 0, tiled=True)


def exchange_near(x):
    groups = [[4 * y + 2 * z + (z ^ side) for y in range(4) for z in range(2)] for side in range(2)]
    return lax.all_to_all(x, ("yh", "zh", "zlh"), 0, 0, tiled=True, axis_index_groups=groups)


def spread(x, count):
    return jnp.broadcast_to(x[None], (count,) + x.shape)


def swap(x):
    return lax.ppermute(x, "c", SWAP)


def gather_block(column):
    main = column[:, :4].transpose(1, 0, 2, 3).reshape(4 * SPAN, 128)
    tail = lax.dynamic_slice_in_dim(column[:, 4], lax.axis_index("x") % 2 * 4, 4, axis=0)
    return jnp.concatenate([main, tail.reshape(SPAN // 2, 128)], axis=0)


def by_row(block):
    main = block[: 4 * SPAN].reshape(4, 8, ROWS, 128).transpose(1, 0, 2, 3)
    tail = block[4 * SPAN :].reshape(4, 1, ROWS, 128)
    zero = jnp.zeros_like(tail)
    low = lax.axis_index("x") % 2 == 0
    tail = jnp.concatenate([jnp.where(low, tail, zero), jnp.where(low, zero, tail)], axis=0)
    return jnp.concatenate([main, tail], axis=1)


def join_units(units):
    main = units[:, :4].reshape(16, ROWS, 128)
    tail = units[:, 4].reshape(2, 2, ROWS, 128).sum(axis=1)
    whole = jnp.concatenate([main, tail], axis=0)
    return whole.transpose(1, 0, 2).reshape(ROWS, 3 * D)


def row_order():
    place = jnp.arange(D, dtype=jnp.int32)
    core = lax.axis_index("c").astype(jnp.int32)
    core = jnp.where(place < HALF, core, 1 - core)
    inner = place % HALF
    low, y_high, z_high, row = inner // SPAN, inner % SPAN // 48, inner % 48 // ROWS, inner % ROWS
    return ((((z_high * 4 + y_high) * 2 + low) * 2 + core) * ROWS + row)[None]


def add_up(own, other, first, second):
    total = (own.astype(F32) + swap(other).astype(F32)).astype(BF)
    shares = exchange(total, ("yl", "x"))
    shares, first = lax.optimization_barrier((shares, first))
    total = jnp.sum(shares.astype(F32), axis=0).astype(BF)
    shares = exchange_near(by_row(total))
    shares, second = lax.optimization_barrier((shares, second))
    total = jnp.sum(shares.astype(F32), axis=0).astype(BF)
    shares = exchange(spread(total, 16), ("x", "zlh", "zll"))
    total = jnp.sum(shares.astype(F32).reshape(4, 4, 5, ROWS, 128), axis=1)
    return join_units(total), first, second


def tokens(x):
    return x.transpose(1, 0, 2).reshape(L_ALL, D)


def crops(x):
    return x.reshape(L_ALL // 2, 2, D).transpose(1, 0, 2)


def on_device(
    student_global,
    student_local,
    teacher_global,
    grad_global,
    grad_local,
    student_qkv,
    teacher_qkv,
    first_moment,
    second_moment,
):
    order = row_order()
    place = lax.axis_index("x").astype(jnp.int32)[None]
    columns = exchange_near(cut(place, student_qkv, teacher_qkv))
    local, grad_rows = tokens(student_local), tokens(grad_local)
    shelf = pre(student_global[0], local, grad_global[0], grad_rows, order)
    columns, shelf = lax.optimization_barrier((columns, shelf))
    student_own = exchange(spread(gather_block(columns[:, 0]), 8), ("yl", "x"))
    student_other = swap(student_own)
    shelf, out_g, own_term, other_term = student(shelf, student_own, student_other)
    out_l = shelf[AT_OL : AT_OL + L_ALL]
    teacher_own = exchange(spread(gather_block(columns[:, 1]), 8), ("yl", "x"))
    teacher_other = swap(teacher_own)
    teacher_rows = teacher(teacher_global[0], order, teacher_own, teacher_other)
    back_g, back_l = post(shelf, student_own, student_other, student_global[0], local, order)

    gradient, (back_g, back_l, out_l), teacher_rows = add_up(
        own_term, other_term, (back_g, crops(back_l), crops(out_l)), teacher_rows
    )
    gradient = gradient * (1.0 / jnp.sqrt(jnp.float32(TOKENS)))
    new_student, new_teacher, new_first, new_second = adam_update(
        student_qkv, teacher_qkv, first_moment, second_moment, gradient
    )
    return (
        out_g[None],
        out_l,
        teacher_rows[None],
        back_g[None],
        back_l,
        new_student,
        new_teacher,
        new_first,
        new_second,
    )


def solution(mesh):
    mesh = Mesh(mesh.devices.reshape(2, 4, 2, 2, 2, 2, 4), AXES)
    crop, rows = P(AXES, None, None), P(FSDP, None)
    return jax.shard_map(
        on_device,
        mesh=mesh,
        in_specs=(crop,) * 5 + (rows,) * 4,
        out_specs=(crop,) * 5 + (rows,) * 4,
        check_vma=False,
    )
```

```python
import jax
import jax.numpy as jnp
from jax import lax
from jax.experimental import pallas as pl
from jax.experimental.pallas import tpu as pltpu
from jax.sharding import Mesh, PartitionSpec as P

HEADS = 12
D = 768
G_TOK = 257
LOCAL_AT = 272
L_ALL = 74
ROWS_S = 352
ROWS_T = 272
KEYS = 384
PAIRS = 6
MAIN = 512
SPAN = 192
BLOCK = 4 * SPAN + SPAN // 2
HALF = 384
AT_N, AT_DO, AT_NT, AT_DP, AT_OL, SHELF = 0, 352, 704, 1472, 2528, 16384
NT = (((1,), (1,)), ((), ()))
NN = (((1,), (0,)), ((), ()))
TN = (((0,), (0,)), ((), ()))
norm_eps = 1e-06
BF = jnp.bfloat16
F32 = jnp.float32


def dot(a, b, dims):
    return lax.dot_general(a, b, dims, preferred_element_type=jnp.float32)


def normalize(x):
    x = x.astype(jnp.float32)
    centred = x - jnp.mean(x, axis=-1, keepdims=True)
    scale = lax.rsqrt(jnp.mean(centred * centred, axis=-1, keepdims=True) + norm_eps)
    return centred * scale, scale


def one_hot(order_ref):
    row = lax.broadcasted_iota(jnp.int32, (D, D), 0)
    return jnp.where(row == order_ref[...], 1.0, 0.0).astype(jnp.bfloat16)


def assemble(src, at, w_ref):
    for g in range(4):
        for low in range(2):
            block, top = 4 * low + g, at + low * SPAN
            for u in range(4):
                w_ref[top : top + SPAN, g * MAIN + u * 128 : g * MAIN + (u + 1) * 128] = src[
                    block, u * SPAN : (u + 1) * SPAN, :
                ]
            top, left = top + (g % 2) * (SPAN // 2), 4 * MAIN + (g // 2) * 128
            w_ref[top : top + SPAN // 2, left : left + 128] = src[block, 4 * SPAN :, :]


def project(n_ref, w_ref, p_ref):
    for part in range(3):
        at = slice(part * D, (part + 1) * D)
        p_ref[:, at] = dot(n_ref[...], w_ref[:, at], NN).astype(jnp.bfloat16)


def doubled(x, first):
    rows = x.shape[0]
    zero = jnp.zeros_like(x)
    pad = jnp.zeros((KEYS - rows, 128), x.dtype)
    return jnp.concatenate([jnp.where(first, x, zero), pad, jnp.where(first, zero, x), pad], axis=0)


def bias_of(shape, keys):
    q = lax.broadcasted_iota(jnp.int32, shape, 1 - keys)
    k = lax.broadcasted_iota(jnp.int32, shape, keys)
    in_global = (q < LOCAL_AT) & (k < G_TOK)
    in_local = (q >= LOCAL_AT) & (k >= LOCAL_AT) & (k < LOCAL_AT + L_ALL) & (q % 2 == k % 2)
    return jnp.where(in_global | in_local, 0.0, -1e30)


def softmax(scores, bias, keys):
    e = jnp.exp(scores + bias)
    return e * (1.0 / jnp.sum(e, axis=keys, keepdims=True))


def copies(pairs, sem):
    return [pltpu.make_async_copy(a, b, sem.at[i]) for i, (a, b) in enumerate(pairs)]


def start(moves):
    for move in moves:
        move.start()


def wait(moves):
    for move in moves:
        move.wait()


def cut_kernel(place_ref, sw_ref, tw_ref, out_ref):
    place = place_ref[0]
    main = pl.ds(pl.multiple_of(place * MAIN, MAIN), MAIN)
    tail = pl.ds(pl.multiple_of(4 * MAIN + place // 2 * 128, 128), 128)
    for i, ref in enumerate((sw_ref, tw_ref)):
        units = ref[:, main].astype(jnp.bfloat16)
        last = ref[:, tail].astype(jnp.bfloat16)
        for copy in range(8):
            for u in range(4):
                out_ref[copy, i, u] = units[:, u * 128 : (u + 1) * 128]
            out_ref[copy, i, 4] = last


def pre_kernel(xg_ref, xl_ref, gg_ref, gl_ref, order_ref, shelf, scr, n_ref, nt_ref, do_ref, sem):
    do_ref[...] = jnp.zeros_like(do_ref)
    do_ref[:G_TOK, :] = gg_ref[...]
    do_ref[LOCAL_AT : LOCAL_AT + L_ALL, :] = gl_ref[...]
    scr[...] = jnp.zeros_like(scr)
    scr[:G_TOK, :] = normalize(xg_ref[...])[0].astype(BF)
    scr[LOCAL_AT : LOCAL_AT + L_ALL, :] = normalize(xl_ref[...])[0].astype(BF)
    n = dot(scr[...], one_hot(order_ref), NN)
    n_ref[...] = n.astype(BF)
    nt_ref[...] = jnp.zeros_like(nt_ref)
    nt_ref[:, :ROWS_S] = n.T.astype(BF)
    moves = copies(
        [
            (n_ref, shelf.at[pl.ds(AT_N, ROWS_S), :]),
            (do_ref, shelf.at[pl.ds(AT_DO, ROWS_S), :]),
            (nt_ref, shelf.at[pl.ds(AT_NT, D), pl.ds(0, KEYS)]),
        ],
        sem,
    )
    start(moves)
    wait(moves)


def student_kernel(
    shelf_in, wo_ref, wx_ref,
    shelf, og_ref, dwo_ref, dwx_ref,
    n_ref, do_scr, nt_ref, ol_ref, dp_ref,
    p_scr, w_scr, bias_scr, sem,
):
    loads = copies(
        [
            (shelf_in.at[pl.ds(AT_N, ROWS_S), :], n_ref),
            (shelf_in.at[pl.ds(AT_DO, ROWS_S), :], do_scr),
            (shelf_in.at[pl.ds(AT_NT, D), pl.ds(0, KEYS)], nt_ref),
        ],
        sem,
    )
    start(loads)
    bias_scr[...] = bias_of((KEYS, ROWS_S), 0)
    ol_ref[...] = jnp.zeros_like(ol_ref)
    assemble(wo_ref, 0, w_scr)
    assemble(wx_ref, HALF, w_scr)
    wait(loads)
    project(n_ref, w_scr, p_scr)
    first = lax.broadcasted_iota(jnp.int32, (ROWS_S, 128), 1) < 64

    @pl.loop(0, PAIRS, unroll=PAIRS)
    def _(i):
        at = [pl.ds(pl.multiple_of(part * D + i * 128, 128), 128) for part in range(3)]
        q, k, v = (p_scr[:, a] for a in at)
        do = do_scr[:, at[0]]
        kd = doubled(k * jnp.bfloat16(0.125), first)
        vd = doubled(v, first)
        scores = dot(kd, q, NT)
        dprob = dot(vd, do, NT)
        bias = bias_scr[...]
        p, ds = [], []
        for h in range(2):
            at_h = slice(h * KEYS, (h + 1) * KEYS)
            prob = softmax(scores[at_h], bias, 0)
            both = prob * dprob[at_h]
            p.append(prob.astype(BF))
            ds.append((both - prob * jnp.sum(both, axis=0, keepdims=True)).astype(BF))
        p = jnp.concatenate(p, axis=0)
        ds = jnp.concatenate(ds, axis=0)
        dv = dot(p, do, NN)
        dk = dot(ds, q * jnp.bfloat16(0.125), NN)
        o = dot(p, vd, TN)
        dq = dot(ds, kd, TN)
        o = o.astype(jnp.bfloat16)
        og_ref[:, at[0]] = o[:G_TOK]
        ol_ref[:L_ALL, at[0]] = o[LOCAL_AT : LOCAL_AT + L_ALL]
        dp_ref[:, at[0]] = dq.astype(jnp.bfloat16)
        dp_ref[:, at[1]] = jnp.where(first, dk[:ROWS_S], dk[KEYS : KEYS + ROWS_S]).astype(jnp.bfloat16)
        dp_ref[:, at[2]] = jnp.where(first, dv[:ROWS_S], dv[KEYS : KEYS + ROWS_S]).astype(jnp.bfloat16)

    pairs = [(ol_ref, shelf.at[pl.ds(AT_OL, 80), :])]
    pairs += [
        (dp_ref.at[:, pl.ds(i * D, D)], shelf.at[pl.ds(AT_DP + i * ROWS_S, ROWS_S), :]) for i in range(3)
    ]
    stores = copies(pairs, sem)
    start(stores)
    for out_ref, rows in ((dwx_ref, slice(HALF, D)), (dwo_ref, slice(0, HALF))):
        nt = nt_ref[rows, :ROWS_S]
        for g in range(4):
            term = dot(nt, dp_ref[:, g * MAIN : (g + 1) * MAIN], NN).astype(jnp.bfloat16)
            for low in range(2):
                for u in range(4):
                    out_ref[4 * low + g, u * SPAN : (u + 1) * SPAN, :] = term[
                        low * SPAN : (low + 1) * SPAN, u * 128 : (u + 1) * 128
                    ]
        term = dot(nt, dp_ref[:, 4 * MAIN :], NN).astype(jnp.bfloat16)
        for g in range(4):
            for low in range(2):
                top, left = low * SPAN + (g % 2) * (SPAN // 2), (g // 2) * 128
                out_ref[4 * low + g, 4 * SPAN :, :] = term[top : top + SPAN // 2, left : left + 128]
    wait(stores)


def post_kernel(
    shelf, xg_ref, xl_ref, wo_ref, wx_ref, order_ref, bg_ref, bl_ref,
    dp_ref, w_scr, sem,
):
    pairs = [
        (shelf.at[pl.ds(AT_DP + i * ROWS_S, ROWS_S), :], dp_ref.at[:, pl.ds(i * D, D)]) for i in range(3)
    ]
    loads = copies(pairs, sem)
    start(loads)
    assemble(wo_ref, 0, w_scr)
    assemble(wx_ref, HALF, w_scr)
    wait(loads)
    dn = dot(dp_ref[...], w_scr[...], NT).astype(jnp.bfloat16)
    dn = dot(dn, one_hot(order_ref), NT)
    for x_ref, out_ref, at, count in ((xg_ref, bg_ref, 0, G_TOK), (xl_ref, bl_ref, LOCAL_AT, L_ALL)):
        hat, scale = normalize(x_ref[...])
        d = dn[at : at + count]
        mean = jnp.mean(d, axis=-1, keepdims=True)
        along = jnp.mean(d * hat, axis=-1, keepdims=True)
        out_ref[...] = (scale * (d - mean - hat * along)).astype(jnp.bfloat16)


def teacher_kernel(x_ref, order_ref, wo_ref, wx_ref, o_ref, n_scr, scr, p_scr, w_scr, bias_scr):
    assemble(wo_ref, 0, w_scr)
    assemble(wx_ref, HALF, w_scr)
    bias_scr[...] = bias_of((ROWS_T, KEYS), 1)
    scr[...] = jnp.zeros_like(scr)
    scr[:G_TOK, :] = normalize(x_ref[...])[0].astype(jnp.bfloat16)
    n_scr[...] = dot(scr[...], one_hot(order_ref), NN).astype(jnp.bfloat16)
    project(n_scr, w_scr, p_scr)
    first = lax.broadcasted_iota(jnp.int32, (ROWS_T, 128), 1) < 64

    @pl.loop(0, PAIRS, unroll=PAIRS)
    def _(i):
        at = [pl.ds(pl.multiple_of(part * D + i * 128, 128), 128) for part in range(3)]
        q, k, v = (p_scr[:, a] for a in at)
        scores = dot(q, doubled(k * jnp.bfloat16(0.125), first), NT)
        bias = bias_scr[...]
        p = [softmax(scores[:, h * KEYS : (h + 1) * KEYS], bias, 1).astype(jnp.bfloat16) for h in range(2)]
        o = dot(jnp.concatenate(p, axis=1), doubled(v, first), NN)
        o_ref[:, at[0]] = o[:G_TOK].astype(jnp.bfloat16)


HBM = pl.BlockSpec(memory_space=pltpu.HBM)
HERE = pl.BlockSpec(memory_space=pltpu.VMEM)


def call(kernel, mib, ins, outs, scratch, sems, flops, nbytes, *args, aliases=None):
    scratch = [pltpu.VMEM(s, t) for s, t in scratch]
    return pl.pallas_call(
        kernel,
        in_specs=ins,
        out_specs=[spec for _, spec in outs],
        out_shape=[jax.ShapeDtypeStruct(s, BF) for s, _ in outs],
        scratch_shapes=scratch + [pltpu.SemaphoreType.DMA((n,)) for n in sems],
        input_output_aliases=aliases or {},
        compiler_params=pltpu.CompilerParams(vmem_limit_bytes=mib * 2**20),
        cost_estimate=pl.CostEstimate(flops=flops, bytes_accessed=nbytes, transcendentals=0),
    )(*args)


def cut(place, sw, tw):
    ins = [pl.BlockSpec(memory_space=pltpu.SMEM), HERE, HERE]
    return call(cut_kernel, 56, ins, [((8, 2, 5, 24, 128), HERE)], [], [], 10**6, 10**6, place, sw, tw)[0]


SHELF_SHAPE = (SHELF, D)


def pre(xg, xl, gg, gl, order):
    here = [((ROWS_S, D), BF), ((ROWS_S, D), BF), ((D, KEYS), BF), ((ROWS_S, D), BF)]
    return call(
        pre_kernel, 44, [HERE] * 5, [(SHELF_SHAPE, HBM)], here, [3],
        10**9, 10**6, xg, xl, gg, gl, order,
    )[0]


def student(shelf, wo, wx):
    block = (8, BLOCK, 128)
    outs = [(SHELF_SHAPE, HBM), ((G_TOK, D), HERE), (block, HERE), (block, HERE)]
    here = [(ROWS_S, D), (ROWS_S, D), (D, KEYS), (80, D)]
    here += [(ROWS_S, 3 * D), (ROWS_S, 3 * D), (D, 3 * D)]
    return call(
        student_kernel, 42, [HBM, HERE, HERE], outs, [(s, BF) for s in here] + [((KEYS, ROWS_S), F32)], [5],
        8 * 10**9, 10**7, shelf, wo, wx, aliases={0: 0},
    )


def post(shelf, wo, wx, xg, xl, order):
    outs = [((G_TOK, D), HERE), ((L_ALL, D), HERE)]
    here = [((ROWS_S, 3 * D), BF), ((D, 3 * D), BF)]
    return call(
        post_kernel, 42, [HBM] + [HERE] * 5, outs, here, [5],
        3 * 10**9, 6 * 10**6, shelf, xg, xl, wo, wx, order,
    )


def teacher(x, order, wo, wx):
    here = [((ROWS_T, D), BF), ((ROWS_T, D), BF), ((ROWS_T, 3 * D), BF)]
    here += [((D, 3 * D), BF), ((ROWS_T, KEYS), F32)]
    return call(
        teacher_kernel, 20, [HERE] * 4, [((G_TOK, D), HERE)], here, [],
        3 * 10**9, 5 * 10**6, x, order, wo, wx,
    )[0]


ROWS = 24
AXES = ("zh", "yh", "yl", "c", "zlh", "zll", "x")
FSDP = ("zh", "yh", "yl", "c")
SWAP = [(0, 1), (1, 0)]
TOKENS = 169472

beta_one = 0.9
beta_two = 0.999
corr_one = 1.0 - 0.9**10
corr_two = 1.0 - 0.999**10
learn_rate = 0.002
decay_rate = 0.04
momentum = 0.994
adam_eps = 1e-08


def adam_update(weight, teacher_weight, first, second, gradient):
    first = beta_one * first + (1.0 - beta_one) * gradient
    second = beta_two * second + (1.0 - beta_two) * gradient * gradient
    update = first / corr_one / (jnp.sqrt(second / corr_two) + adam_eps)
    weight_new = weight - learn_rate * (update + decay_rate * weight)
    teacher_new = momentum * teacher_weight + (1.0 - momentum) * weight_new
    return (weight_new, teacher_new, first, second)


def exchange(x, axes):
    return lax.all_to_all(x, axes, 0, 0, tiled=True)


def exchange_near(x):
    groups = [[4 * y + 2 * z + (z ^ side) for y in range(4) for z in range(2)] for side in range(2)]
    return lax.all_to_all(x, ("yh", "zh", "zlh"), 0, 0, tiled=True, axis_index_groups=groups)


def spread(x, count):
    return jnp.broadcast_to(x[None], (count,) + x.shape)


def swap(x):
    return lax.ppermute(x, "c", SWAP)


def gather_block(column):
    main = column[:, :4].transpose(1, 0, 2, 3).reshape(4 * SPAN, 128)
    tail = lax.dynamic_slice_in_dim(column[:, 4], lax.axis_index("x") % 2 * 4, 4, axis=0)
    return jnp.concatenate([main, tail.reshape(SPAN // 2, 128)], axis=0)


def by_row(block):
    main = block[: 4 * SPAN].reshape(4, 8, ROWS, 128).transpose(1, 0, 2, 3)
    tail = block[4 * SPAN :].reshape(4, 1, ROWS, 128)
    zero = jnp.zeros_like(tail)
    low = lax.axis_index("x") % 2 == 0
    tail = jnp.concatenate([jnp.where(low, tail, zero), jnp.where(low, zero, tail)], axis=0)
    return jnp.concatenate([main, tail], axis=1)


def join_units(units):
    main = units[:, :4].reshape(16, ROWS, 128)
    tail = units[:, 4].reshape(2, 2, ROWS, 128).sum(axis=1)
    whole = jnp.concatenate([main, tail], axis=0)
    return whole.transpose(1, 0, 2).reshape(ROWS, 3 * D)


def row_order():
    place = jnp.arange(D, dtype=jnp.int32)
    core = lax.axis_index("c").astype(jnp.int32)
    core = jnp.where(place < HALF, core, 1 - core)
    inner = place % HALF
    low, y_high, z_high, row = inner // SPAN, inner % SPAN // 48, inner % 48 // ROWS, inner % ROWS
    return ((((z_high * 4 + y_high) * 2 + low) * 2 + core) * ROWS + row)[None]


def add_up(own, other, first, second):
    total = (own.astype(F32) + swap(other).astype(F32)).astype(BF)
    shares = exchange(total, ("yl", "x"))
    shares, first = lax.optimization_barrier((shares, first))
    total = jnp.sum(shares.astype(F32), axis=0).astype(BF)
    shares = exchange_near(by_row(total))
    shares, second = lax.optimization_barrier((shares, second))
    total = jnp.sum(shares.astype(F32), axis=0).astype(BF)
    shares = exchange(spread(total, 16), ("x", "zlh", "zll"))
    total = jnp.sum(shares.astype(F32).reshape(4, 4, 5, ROWS, 128), axis=1)
    return join_units(total), first, second


def tokens(x):
    return x.transpose(1, 0, 2).reshape(L_ALL, D)


def crops(x):
    return x.reshape(L_ALL // 2, 2, D).transpose(1, 0, 2)


def on_device(
    student_global,
    student_local,
    teacher_global,
    grad_global,
    grad_local,
    student_qkv,
    teacher_qkv,
    first_moment,
    second_moment,
):
    order = row_order()
    place = lax.axis_index("x").astype(jnp.int32)[None]
    columns = exchange_near(cut(place, student_qkv, teacher_qkv))
    local, grad_rows = tokens(student_local), tokens(grad_local)
    shelf = pre(student_global[0], local, grad_global[0], grad_rows, order)
    columns, shelf = lax.optimization_barrier((columns, shelf))
    student_own = exchange(spread(gather_block(columns[:, 0]), 8), ("yl", "x"))
    student_other = swap(student_own)
    shelf, out_g, own_term, other_term = student(shelf, student_own, student_other)
    out_l = shelf[AT_OL : AT_OL + L_ALL]
    teacher_own = exchange(spread(gather_block(columns[:, 1]), 8), ("yl", "x"))
    teacher_other = swap(teacher_own)
    teacher_rows = teacher(teacher_global[0], order, teacher_own, teacher_other)
    back_g, back_l = post(shelf, student_own, student_other, student_global[0], local, order)

    gradient, (back_g, back_l, out_l), teacher_rows = add_up(
        own_term, other_term, (back_g, crops(back_l), crops(out_l)), teacher_rows
    )
    gradient = gradient * (1.0 / jnp.sqrt(jnp.float32(TOKENS)))
    new_student, new_teacher, new_first, new_second = adam_update(
        student_qkv, teacher_qkv, first_moment, second_moment, gradient
    )
    return (
        out_g[None],
        out_l,
        teacher_rows[None],
        back_g[None],
        back_l,
        new_student,
        new_teacher,
        new_first,
        new_second,
    )


def solution(mesh):
    mesh = Mesh(mesh.devices.reshape(2, 4, 2, 2, 2, 2, 4), AXES)
    crop, rows = P(AXES, None, None), P(FSDP, None)
    return jax.shard_map(
        on_device,
        mesh=mesh,
        in_specs=(crop,) * 5 + (rows,) * 4,
        out_specs=(crop,) * 5 + (rows,) * 4,
        check_vma=False,
    )
```
